32 devices in a mesh: row: 4 (over y, core), col: 8 (over z, x).
Axes of the slice: x: 2, y: 2, z: 4, core: 2. Of those that a mesh axis runs over, the one named last changes fastest.
Arguments:
- points: float32 [3, 4, 8192], P(None, None, ('row', 'col')), may hold values from 0 to 1
- weights: float32 [4, 8192], P(None, ('row', 'col')), may hold values from 0.05 to 0.2
- shift: float32 [8192], P(('row', 'col')), may hold values from 0.5 to 4
- cluster_rank: int32 [16], replicated, may hold values from 0 to 15, each once
Outputs:
- factor: float32 [4, 4, 512, 2, 8, 512], P(None, 'row', None, None, 'col')
The draws below stay inside these ranges and needn't reach their ends.
Inputs may be any that keep to these rules, and one draw needn't show every extreme that they name: `cluster_rank`: every cluster has a distinct elimination position.
All inputs are finite; a program needn't handle non-finite values.
Results may differ from the reference program's by a relative error of at most 0.0003.
Values sent between devices are 32-bit elements; how exact they have to be, the bound alone decides.
A program may use at most 128 MiB of HBM per device.

```python
import math
import jax
import jax.numpy as jnp
from jax import lax

TILE = 512
QUAD = 4
RB = 4
GRID_ROWS = 4
GRID_COLS = 8
NT = 16
CB = 2
W = 8192


def level_of(rng, extent, pieces, smallest, top_value):
    gain, own = 1.0, jax.random.fold_in(rng, 6)
    for dim, blocks in pieces:
        heights = jnp.exp(jax.random.uniform(jax.random.fold_in(own, dim), (blocks,), jnp.float32, smallest / len(pieces), top_value / len(pieces)))
        gain = gain * jnp.repeat(heights, extent[dim] // blocks).reshape([-1 if axis == dim else 1 for axis in range(len(extent))])
    return gain


def setup_inputs(seed: int = 0) -> dict:
    splits = jax.random.split(jax.random.key(seed), 5)
    return {
        "points": jnp.clip(1.0 * jax.random.uniform(splits[0], (3, QUAD, W), jnp.float32) ** level_of(splits[0], (3, QUAD, W), ((2, 32),), -0.2, 0.2), 0.0, 1.0),
        "weights": jnp.clip(jnp.exp(math.log(0.2) - 1.3862944 * jax.random.uniform(splits[1], (QUAD, W), jnp.float32) ** level_of(splits[1], (QUAD, W), ((1, 32),), -0.2, 0.2)), 0.05, 0.2),
        "shift": jnp.clip(jnp.exp(math.log(4.0) - 2.0794415 * jax.random.uniform(splits[2], (W,), jnp.float32) ** level_of(splits[2], (W,), ((0, 32),), -0.2, 0.2)), 0.5, 4.0),
        "cluster_rank": jax.random.permutation(splits[3], NT).astype(jnp.int32),
    }


SOFTENING_SQUARED = 0.0004

def kernel_block(row_geometry, col_geometry):
    values = jnp.zeros((row_geometry.shape[2], col_geometry.shape[2]), jnp.float32)
    for first in range(row_geometry.shape[1]):
        for second in range(col_geometry.shape[1]):
            squared = SOFTENING_SQUARED
            for coordinate in range(3):
                offset = row_geometry[coordinate, first][:, None] - col_geometry[coordinate, second][None, :]
                squared = squared + offset * offset
            product = row_geometry[3, first][:, None] * col_geometry[3, second][None, :]
            values = values + product * lax.rsqrt(squared)
    return values

def reorder(points, weights, shift, cluster_rank):
    clusters = cluster_rank.shape[0]
    positions = jnp.arange(clusters, dtype=jnp.int32)
    order = lax.optimization_barrier(jnp.sum(jnp.where(cluster_rank[None, :] == positions[:, None], positions[None, :], 0), axis=1)).astype(jnp.int32)
    geometry = jnp.concatenate([points, weights[None]], axis=0)
    quadrature = geometry.shape[1]
    geometry = geometry.reshape(4, quadrature, clusters, -1)
    geometry = jnp.take(geometry, order, axis=2).reshape(4, quadrature, -1)
    shifted = jnp.take(shift.reshape(clusters, -1), order, axis=0).reshape(-1)
    return (geometry, shifted)

def reference(points, weights, shift, cluster_rank):
    geometry, shifted = reorder(points, weights, shift, cluster_rank)

    def row_block(start):
        rows = lax.dynamic_slice_in_dim(geometry, start, TILE, 2)
        return kernel_block(rows, geometry)
    starts = (jnp.arange(NT, dtype=jnp.int32) * TILE).astype(jnp.int32)
    matrix = lax.map(row_block, starts).reshape(W, W)
    diagonal_index = jnp.arange(W, dtype=jnp.int32)
    matrix = matrix.at[diagonal_index, diagonal_index].add(shifted)
    for step in range(2):
        begin = step * TILE
        end = begin + TILE
        diagonal_factor = jnp.linalg.cholesky(matrix[begin:end, begin:end])
        panel = lax.linalg.triangular_solve(diagonal_factor, matrix[end:, begin:end], left_side=False, lower=True, transpose_a=True)
        update = jnp.dot(panel, panel.T, precision=lax.Precision.HIGHEST)
        matrix = matrix.at[end:, end:].add(-update)
        matrix = matrix.at[begin:end, begin:end].set(diagonal_factor)
        matrix = matrix.at[end:, begin:end].set(panel)
    tiles = matrix.reshape(NT, TILE, NT, TILE)
    tile_index = jnp.arange(NT, dtype=jnp.int32)
    keep = tile_index[:, None] >= tile_index[None, :]
    tiles = jnp.where(keep[:, None, :, None], tiles, 0.0)
    return tiles.reshape(RB, GRID_ROWS, TILE, CB, GRID_COLS, TILE)
```

```python
import functools

import jax
import jax.numpy as jnp
from jax import lax
from jax.experimental import pallas as pl
from jax.experimental.pallas import tpu as pltpu
from jax.sharding import PartitionSpec as P

SOFTENING_SQUARED = 0.0004
HIGHEST = lax.Precision.HIGHEST
FEATURES = 48
BLOCK = 128
ROWS = 64


def gather_kernel(row_count, col_count, own, out, local_sem, send_col, recv_col, send_row, recv_row):
    row = lax.axis_index("row")
    col = lax.axis_index("col")
    barrier = pltpu.get_barrier_semaphore()
    for step in range(1, col_count):
        peer = lax.rem(col + step, col_count)
        pl.semaphore_signal(barrier, inc=1, device_id={"col": peer}, device_id_type=pl.DeviceIdType.MESH)
    for step in range(1, row_count):
        peer = lax.rem(row + step, row_count)
        pl.semaphore_signal(barrier, inc=1, device_id={"row": peer}, device_id_type=pl.DeviceIdType.MESH)
    pl.semaphore_wait(barrier, row_count + col_count - 2)
    keep = pltpu.make_async_copy(own, out.at[row, col], local_sem)
    keep.start()
    copies = []
    for step in range(1, col_count):
        peer = lax.rem(col + step, col_count)
        copies.append(
            pltpu.make_async_remote_copy(
                src_ref=own,
                dst_ref=out.at[row, col],
                send_sem=send_col.at[step - 1],
                recv_sem=recv_col.at[step - 1],
                device_id={"col": peer},
                device_id_type=pl.DeviceIdType.MESH,
            )
        )
        copies[-1].start()
    keep.wait()
    for copy in copies:
        copy.wait()
    copies = []
    for step in range(1, row_count):
        peer = lax.rem(row + step, row_count)
        copies.append(
            pltpu.make_async_remote_copy(
                src_ref=out.at[row],
                dst_ref=out.at[row],
                send_sem=send_row.at[step - 1],
                recv_sem=recv_row.at[step - 1],
                device_id={"row": peer},
                device_id_type=pl.DeviceIdType.MESH,
            )
        )
        copies[-1].start()
    for copy in copies:
        copy.wait()


def gather(own, row_count, col_count):
    return pl.pallas_call(
        functools.partial(gather_kernel, row_count, col_count),
        out_shape=jax.ShapeDtypeStruct((row_count, col_count) + own.shape, own.dtype),
        in_specs=[pl.BlockSpec(memory_space=pltpu.VMEM)],
        out_specs=pl.BlockSpec(memory_space=pltpu.VMEM),
        scratch_shapes=[
            pltpu.SemaphoreType.DMA,
            pltpu.SemaphoreType.DMA((col_count - 1,)),
            pltpu.SemaphoreType.DMA((col_count - 1,)),
            pltpu.SemaphoreType.DMA((row_count - 1,)),
            pltpu.SemaphoreType.DMA((row_count - 1,)),
        ],
        compiler_params=pltpu.CompilerParams(collective_id=0, has_side_effects=True),
        name="gather_panels",
    )(own)


def dot(left, right, precision=None):
    return lax.dot_general(
        left, right, (((1,), (0,)), ((), ())), precision=precision, preferred_element_type=jnp.float32
    )


def dot_transposed(left, right, precision=None):
    return lax.dot_general(
        left, right, (((1,), (1,)), ((), ())), precision=precision, preferred_element_type=jnp.float32
    )


def split(value):
    high = value.astype(jnp.bfloat16)
    return high, (value - high.astype(jnp.float32)).astype(jnp.bfloat16)


def factor_block(source, upper, inverse, side):
    row_ids = lax.broadcasted_iota(jnp.int32, (BLOCK, BLOCK), 0)
    col_ids = lax.broadcasted_iota(jnp.int32, (BLOCK, BLOCK), 1)
    eight = lax.broadcasted_iota(jnp.int32, (8, BLOCK), 0)
    empty = jnp.zeros((8, BLOCK), jnp.float32)

    def panel(index, state):
        values, companion = state
        side(index)
        upper_rows, inverse_rows = empty, empty
        for j in range(8):
            scale = lax.rsqrt(values[j : j + 1, j : j + 1])
            pivot_row = values[j : j + 1, :] * scale
            companion_row = companion[j : j + 1, :] * scale
            column = jnp.broadcast_to(values[:, j : j + 1], (BLOCK, BLOCK)) * scale
            column = jnp.where(row_ids > j, column, 0.0)
            upper_rows = jnp.where(eight == j, pivot_row, upper_rows)
            inverse_rows = jnp.where(eight == j, companion_row, inverse_rows)
            values = values - column * pivot_row
            companion = companion - column * companion_row
        start = pl.multiple_of(index * 8, 8)
        upper[pl.ds(start, 8), :] = pltpu.roll(upper_rows, start, 1)
        inverse[pl.ds(start, 8), :] = inverse_rows
        values = pltpu.roll(jnp.concatenate([values[8:], empty], axis=0), BLOCK - 8, 1)
        companion = jnp.concatenate([companion[8:], empty], axis=0)
        return values, companion

    identity = jnp.where(row_ids == col_ids, 1.0, 0.0)
    lax.fori_loop(0, BLOCK // 8, panel, (source, identity))
    return jnp.where(col_ids >= row_ids, upper[...], 0.0).T, inverse[...]


def factor_tile(matrix, lower, inverse, upper_block, inverse_block, side):
    tile = matrix.shape[0]
    count = tile // BLOCK
    lower[...] = jnp.zeros((tile, tile), jnp.float32)
    inverse[...] = jnp.zeros((tile, tile), jnp.float32)
    for k in range(count):
        here = slice(k * BLOCK, (k + 1) * BLOCK)
        below = slice((k + 1) * BLOCK, tile)
        first = k * (BLOCK // 8)
        diagonal, block = factor_block(
            matrix[here, here], upper_block, inverse_block, lambda index: side(first + index)
        )
        lower[here, here] = diagonal
        inverse[here, here] = block
        if k + 1 < count:
            solved = dot_transposed(matrix[below, here], block, HIGHEST)
            lower[below, here] = solved
            matrix[below, below] = matrix[below, below] - dot_transposed(solved, solved, HIGHEST)
    size = BLOCK
    while size < tile:
        for start in range(0, tile, 2 * size):
            top = slice(start, start + size)
            bottom = slice(start + size, start + 2 * size)
            inner = dot(lower[bottom, top], inverse[top, top], HIGHEST)
            inverse[bottom, top] = -dot(inverse[bottom, bottom], inner, HIGHEST)
        size *= 2


def main_kernel(
    row_tiles, col_tiles, own_count,
    plan, own_plan, left, right, exact,
    out,
    tiles, matrix, lower0, lower1, inverse, inverse_high, inverse_low, first_high, first_low,
    panel_high, panel_low, upper_block, inverse_block,
):
    tile = matrix.shape[0]
    quadrature = right.shape[1]
    chunks = tile // ROWS
    listed = 2 + row_tiles + col_tiles
    work = plan.shape[0] // 4

    def assemble(item, chunk):
        left_index, right_index = plan[4 * item], plan[4 * item + 1]
        diagonal = plan[4 * item + 2]
        start = pl.multiple_of(chunk * ROWS, ROWS)
        row_ids = lax.broadcasted_iota(jnp.int32, (ROWS, tile), 0) + start
        col_ids = lax.broadcasted_iota(jnp.int32, (ROWS, tile), 1)
        on_diagonal = (row_ids - col_ids) == jnp.where(diagonal == 1, 0, 2 * tile)
        features = left[left_index, chunk]
        total = jnp.zeros((ROWS, tile), jnp.float32)
        for second in range(quadrature):
            squared = dot(features, right[right_index, second])
            for first in range(quadrature):
                part = squared[first * ROWS : (first + 1) * ROWS]
                if first == second:
                    part = jnp.where(on_diagonal, exact[right_index, second : second + 1, :], part)
                total = total + lax.rsqrt(part)
        shifted = exact[right_index, quadrature : quadrature + 1, :]
        tiles[item, pl.ds(start, ROWS), :] = total + jnp.where(on_diagonal, shifted, 0.0)

    def assemble_tile(item):
        def step(chunk, carry):
            assemble(item, chunk)
            return carry
        lax.fori_loop(0, chunks, step, 0)

    def side_from(first_item):
        def side(index):
            assemble(first_item + index // chunks, lax.rem(index, chunks))
        return side

    panels = tile // 8
    covered = panels // chunks
    assemble_tile(0)
    matrix[...] = tiles[0]
    factor_tile(matrix, lower0, inverse, upper_block, inverse_block, side_from(1))
    inverse_high[0], inverse_low[0] = split(inverse[...].T)

    def three(left_high, left_low, right_high, right_low, multiply):
        return (
            multiply(left_high, right_high)
            + multiply(left_high, right_low)
            + multiply(left_low, right_high)
        )

    def solve_first(index, carry):
        high, low = split(tiles[index])
        solved = three(high, low, inverse_high[0], inverse_low[0], dot)
        high, low = split(solved)
        panel_high[index - 1, :, :tile] = high
        panel_low[index - 1, :, :tile] = low
        return carry

    lax.fori_loop(1, listed, solve_first, 0)
    first_high[...] = panel_high[0, :, :tile]
    first_low[...] = panel_low[0, :, :tile]

    def reduce_second(index, carry):
        update = three(
            panel_high[index - 1, :, :tile], panel_low[index - 1, :, :tile],
            first_high[...], first_low[...], dot_transposed,
        )
        item = listed - 1 + index
        tiles[item] = tiles[item] - update
        return carry

    reduce_second(1, 0)
    matrix[...] = tiles[listed]
    factor_tile(matrix, lower1, inverse, upper_block, inverse_block, side_from(1 + covered))
    inverse_high[1], inverse_low[1] = split(inverse[...].T)
    done = 1 + 2 * covered

    def solve_second(index, carry):
        reduce_second(index, carry)
        high, low = split(tiles[listed - 1 + index])
        solved = three(high, low, inverse_high[1], inverse_low[1], dot)
        high, low = split(solved)
        panel_high[index - 1, :, tile:] = high
        panel_low[index - 1, :, tile:] = low
        return carry

    lax.fori_loop(2, listed, solve_second, 0)

    def rest(item, carry):
        @pl.when(plan[4 * item + 3] == 1)
        def _():
            assemble_tile(item)
        return carry

    lax.fori_loop(done, work, rest, 0)

    lanes = tile // BLOCK
    pitch = col_tiles * lanes

    def store(i, j, value):
        for q in range(lanes):
            out[pl.ds(i * tile * pitch + j * lanes + q, tile, stride=pitch), :] = value[
                :, q * BLOCK : (q + 1) * BLOCK
            ]

    def finish(index, carry):
        i, j = index // col_tiles, lax.rem(index, col_tiles)
        kind = own_plan[2 * index]

        @pl.when(kind == 0)
        def _():
            store(i, j, jnp.zeros((tile, tile), jnp.float32))

        @pl.when(kind == 1)
        def _():
            store(i, j, lower0[...])

        @pl.when(kind == 2)
        def _():
            value = panel_high[1 + i, :, :tile].astype(jnp.float32)
            store(i, j, value + panel_low[1 + i, :, :tile].astype(jnp.float32))

        @pl.when(kind == 3)
        def _():
            store(i, j, lower1[...])

        @pl.when(kind == 4)
        def _():
            value = panel_high[1 + i, :, tile:].astype(jnp.float32)
            store(i, j, value + panel_low[1 + i, :, tile:].astype(jnp.float32))

        @pl.when(kind == 5)
        def _():
            update = three(
                panel_high[1 + i], panel_low[1 + i],
                panel_high[1 + row_tiles + j], panel_low[1 + row_tiles + j], dot_transposed,
            )
            store(i, j, tiles[own_plan[2 * index + 1]] - update)

        return carry

    lax.fori_loop(0, row_tiles * col_tiles, finish, 0)


def pieces(value):
    parts = []
    for _ in range(3):
        part = lax.reduce_precision(value, 8, 7)
        parts.append(part)
        value = value - part
    return parts


def shards(points, weights, shift, cluster_rank):
    row_count = lax.axis_size("row")
    col_count = lax.axis_size("col")
    row_index = lax.axis_index("row")
    col_index = lax.axis_index("col")
    quadrature, length = weights.shape
    clusters = cluster_rank.shape[0]
    tile = length * row_count * col_count // clusters
    row_tiles = clusters // row_count
    col_tiles = clusters // col_count

    own = jnp.concatenate([points.reshape(3 * quadrature, length), weights, shift[None]], axis=0)
    rows = own.shape[0]
    own = jnp.pad(own, ((0, -rows % 8), (0, 0)))
    everything = gather(own, row_count, col_count)

    block_rows = jnp.arange(row_tiles, dtype=jnp.int32) * row_count + row_index
    block_cols = jnp.arange(col_tiles, dtype=jnp.int32) * col_count + col_index
    places = jnp.concatenate([jnp.arange(2, dtype=jnp.int32), block_rows, block_cols])
    listed = places.shape[0]
    names = jnp.arange(clusters, dtype=jnp.int32)
    chosen = jnp.sum(
        jnp.where(cluster_rank[None, :] == places[:, None], names[None, :], 0), axis=1
    )
    everything = everything.reshape(clusters, tile // length, -1, length)
    local = jnp.take(everything, chosen, axis=0)[:, :, :rows]
    local = jnp.transpose(local, (2, 0, 1, 3)).reshape(rows, listed, tile)
    coordinates = local[: 3 * quadrature].reshape(3, quadrature, listed, tile) - 0.5
    weight = local[3 * quadrature : 4 * quadrature]
    shifted = local[4 * quadrature]
    scale = 1.0 / (weight * weight)
    norm = jnp.sum(coordinates * coordinates, axis=0)
    left_parts = pieces(
        jnp.concatenate(
            [-2.0 * coordinates * scale, ((norm + SOFTENING_SQUARED) * scale)[None], scale[None]]
        )
    )
    right_parts = pieces(
        jnp.concatenate([coordinates * scale, scale[None], (norm * scale)[None]])
    )
    left = jnp.concatenate([left_parts[i] for i in range(3) for _ in range(3)])
    right = jnp.concatenate([right_parts[i] for _ in range(3) for i in range(3)])
    padding = ((0, FEATURES - left.shape[0]), (0, 0), (0, 0), (0, 0))
    left = jnp.pad(left.astype(jnp.bfloat16), padding)
    right = jnp.pad(right.astype(jnp.bfloat16), padding)
    left = left.reshape(FEATURES, quadrature, listed, tile // ROWS, ROWS)
    left = jnp.transpose(left, (2, 3, 1, 4, 0)).reshape(
        listed, tile // ROWS, quadrature * ROWS, FEATURES
    )
    right = jnp.transpose(right, (2, 1, 0, 3))
    exact = jnp.concatenate([SOFTENING_SQUARED * scale * scale, shifted[None]])
    exact = jnp.pad(jnp.transpose(exact, (1, 0, 2)), ((0, 0), (0, -exact.shape[0] % 8), (0, 0)))

    own_rows = jnp.repeat(jnp.arange(row_tiles, dtype=jnp.int32), col_tiles)
    own_cols = jnp.tile(jnp.arange(col_tiles, dtype=jnp.int32), row_tiles)
    tile_row, tile_col = block_rows[own_rows], block_cols[own_cols]
    active = (tile_row >= tile_col) & (tile_col >= 2)
    own_count = max(
        sum(
            i * row_count + r >= j * col_count + c
            for i in range(row_tiles)
            for j in range(col_tiles)
        )
        for r in range(row_count)
        for c in range(col_count)
    )
    slot = jnp.cumsum(active.astype(jnp.int32)) - 1
    takes = active[None, :] & (slot[None, :] == jnp.arange(own_count, dtype=jnp.int32)[:, None])

    def placed(values):
        return jnp.sum(jnp.where(takes, values[None, :], 0), axis=1)

    ordered = jnp.arange(1, listed, dtype=jnp.int32)
    zero = jnp.zeros((1,), jnp.int32)
    left_index = jnp.concatenate([zero, ordered, ordered, placed(own_rows + 2)])
    right_index = jnp.concatenate(
        [zero, 0 * ordered, 0 * ordered + 1, placed(own_cols + 2 + row_tiles)]
    )
    used = jnp.concatenate(
        [zero + 1, 0 * ordered + 1, 0 * ordered + 1, placed(active.astype(jnp.int32))]
    )
    diagonal = (places[left_index] == places[right_index]).astype(jnp.int32)
    plan = jnp.stack([left_index, right_index, diagonal, used], axis=1).reshape(-1)
    kind = jnp.where(
        tile_row < tile_col, 0,
        jnp.where(
            tile_col >= 2, 5,
            jnp.where(tile_col == 0, jnp.where(tile_row == 0, 1, 2), jnp.where(tile_row == 1, 3, 4)),
        ),
    ).astype(jnp.int32)
    base = 2 * listed - 1
    own_plan = jnp.stack([kind, base + jnp.where(active, slot, 0)], axis=1).reshape(-1).astype(jnp.int32)

    work = base + own_count
    whole = pl.BlockSpec(memory_space=pltpu.VMEM)
    scalars = pl.BlockSpec(memory_space=pltpu.SMEM)
    f32, bf16 = jnp.float32, jnp.bfloat16
    result = pl.pallas_call(
        functools.partial(main_kernel, row_tiles, col_tiles, own_count),
        out_shape=jax.ShapeDtypeStruct((row_tiles * tile * col_tiles * tile // BLOCK, BLOCK), f32),
        in_specs=[scalars, scalars, whole, whole, whole],
        out_specs=whole,
        scratch_shapes=[
            pltpu.VMEM((work, tile, tile), f32),
            pltpu.VMEM((tile, tile), f32),
            pltpu.VMEM((tile, tile), f32),
            pltpu.VMEM((tile, tile), f32),
            pltpu.VMEM((tile, tile), f32),
            pltpu.VMEM((2, tile, tile), bf16),
            pltpu.VMEM((2, tile, tile), bf16),
            pltpu.VMEM((tile, tile), bf16),
            pltpu.VMEM((tile, tile), bf16),
            pltpu.VMEM((listed - 1, tile, 2 * tile), bf16),
            pltpu.VMEM((listed - 1, tile, 2 * tile), bf16),
            pltpu.VMEM((BLOCK, BLOCK), f32),
            pltpu.VMEM((BLOCK, BLOCK), f32),
        ],
        compiler_params=pltpu.CompilerParams(vmem_limit_bytes=63 * 1024 * 1024),
        name="assemble_and_factor",
    )(plan, own_plan, left, right, exact)
    return result.reshape(row_tiles, 1, tile, col_tiles, 1, tile)


def solution(mesh):
    return jax.shard_map(
        shards,
        mesh=mesh,
        in_specs=(P(None, None, ("row", "col")), P(None, ("row", "col")), P(("row", "col")), P()),
        out_specs=P(None, "row", None, None, "col", None),
        check_vma=False,
    )
```

```python
import functools

import jax
import jax.numpy as jnp
from jax import lax
from jax.experimental import pallas as pl
from jax.experimental.pallas import tpu as pltpu
from jax.sharding import PartitionSpec as P

SOFTENING_SQUARED = 0.0004
HIGHEST = lax.Precision.HIGHEST
FEATURES = 32
BLOCK = 128
ROWS = 64


def gather_kernel(row_count, col_count, own, out, local_sem, send_col, recv_col, send_row, recv_row):
    row = lax.axis_index("row")
    col = lax.axis_index("col")
    barrier = pltpu.get_barrier_semaphore()
    for step in range(1, col_count):
        peer = lax.rem(col + step, col_count)
        pl.semaphore_signal(barrier, inc=1, device_id={"col": peer}, device_id_type=pl.DeviceIdType.MESH)
    for step in range(1, row_count):
        peer = lax.rem(row + step, row_count)
        pl.semaphore_signal(barrier, inc=1, device_id={"row": peer}, device_id_type=pl.DeviceIdType.MESH)
    pl.semaphore_wait(barrier, row_count + col_count - 2)
    keep = pltpu.make_async_copy(own, out.at[row, col], local_sem)
    keep.start()
    copies = []
    for step in range(1, col_count):
        peer = lax.rem(col + step, col_count)
        copies.append(
            pltpu.make_async_remote_copy(
                src_ref=own,
                dst_ref=out.at[row, col],
                send_sem=send_col.at[step - 1],
                recv_sem=recv_col.at[step - 1],
                device_id={"col": peer},
                device_id_type=pl.DeviceIdType.MESH,
            )
        )
        copies[-1].start()
    keep.wait()
    for copy in copies:
        copy.wait()
    copies = []
    for step in range(1, row_count):
        peer = lax.rem(row + step, row_count)
        copies.append(
            pltpu.make_async_remote_copy(
                src_ref=out.at[row],
                dst_ref=out.at[row],
                send_sem=send_row.at[step - 1],
                recv_sem=recv_row.at[step - 1],
                device_id={"row": peer},
                device_id_type=pl.DeviceIdType.MESH,
            )
        )
        copies[-1].start()
    for copy in copies:
        copy.wait()


def gather(own, row_count, col_count):
    return pl.pallas_call(
        functools.partial(gather_kernel, row_count, col_count),
        out_shape=jax.ShapeDtypeStruct((row_count, col_count) + own.shape, own.dtype),
        in_specs=[pl.BlockSpec(memory_space=pltpu.VMEM)],
        out_specs=pl.BlockSpec(memory_space=pltpu.VMEM),
        scratch_shapes=[
            pltpu.SemaphoreType.DMA,
            pltpu.SemaphoreType.DMA((col_count - 1,)),
            pltpu.SemaphoreType.DMA((col_count - 1,)),
            pltpu.SemaphoreType.DMA((row_count - 1,)),
            pltpu.SemaphoreType.DMA((row_count - 1,)),
        ],
        compiler_params=pltpu.CompilerParams(collective_id=0, has_side_effects=True),
        name="gather_panels",
    )(own)


def dot(left, right, precision=None):
    return lax.dot_general(
        left, right, (((1,), (0,)), ((), ())), precision=precision, preferred_element_type=jnp.float32
    )


def dot_transposed(left, right, precision=None):
    return lax.dot_general(
        left, right, (((1,), (1,)), ((), ())), precision=precision, preferred_element_type=jnp.float32
    )


def split(value):
    high = value.astype(jnp.bfloat16)
    return high, (value - high.astype(jnp.float32)).astype(jnp.bfloat16)


def factor_block(source, upper, inverse, side):
    row_ids = lax.broadcasted_iota(jnp.int32, (BLOCK, BLOCK), 0)
    col_ids = lax.broadcasted_iota(jnp.int32, (BLOCK, BLOCK), 1)
    eight = lax.broadcasted_iota(jnp.int32, (8, BLOCK), 0)
    empty = jnp.zeros((8, BLOCK), jnp.float32)

    def panel(index, state):
        values, companion = state
        side(index)
        upper_rows, inverse_rows = empty, empty
        for j in range(8):
            column = jnp.broadcast_to(values[:, j : j + 1], values.shape)
            scale = lax.rsqrt(column[j : j + 1, :])
            pivot_row = values[j : j + 1, :] * scale
            companion_row = companion[j : j + 1, :] * scale
            column = column * scale
            column = jnp.concatenate([jnp.where(eight > j, column[:8], 0.0), column[8:]], axis=0)
            upper_rows = jnp.where(eight == j, pivot_row, upper_rows)
            inverse_rows = jnp.where(eight == j, companion_row, inverse_rows)
            values = values - column * pivot_row
            companion = companion - column * companion_row
        start = pl.multiple_of(index * 8, 8)
        upper[pl.ds(start, 8), :] = pltpu.roll(upper_rows, start, 1)
        inverse[pl.ds(start, 8), :] = inverse_rows
        values = pltpu.roll(jnp.concatenate([values[8:], empty], axis=0), BLOCK - 8, 1)
        companion = jnp.concatenate([companion[8:], empty], axis=0)
        return values, companion

    identity = jnp.where(row_ids == col_ids, 1.0, 0.0)
    middle = BLOCK // 16
    values, companion = lax.fori_loop(0, middle, panel, (source, identity))
    live = BLOCK // 2
    lax.fori_loop(middle, 2 * middle, panel, (values[:live], companion[:live]))
    return jnp.where(col_ids >= row_ids, upper[...], 0.0).T, inverse[...]


def factor_tile(matrix, lower, inverse, upper_block, inverse_block, side):
    tile = matrix.shape[0]
    count = tile // BLOCK
    lower[...] = jnp.zeros((tile, tile), jnp.float32)
    inverse[...] = jnp.zeros((tile, tile), jnp.float32)
    for k in range(count):
        here = slice(k * BLOCK, (k + 1) * BLOCK)
        below = slice((k + 1) * BLOCK, tile)
        first = k * (BLOCK // 8)
        diagonal, block = factor_block(
            matrix[here, here], upper_block, inverse_block, lambda index: side(first + index)
        )
        lower[here, here] = diagonal
        inverse[here, here] = block
        if k + 1 < count:
            solved = dot_transposed(matrix[below, here], block, HIGHEST)
            lower[below, here] = solved
            matrix[below, below] = matrix[below, below] - dot_transposed(solved, solved, HIGHEST)
    size = BLOCK
    while size < tile:
        for start in range(0, tile, 2 * size):
            top = slice(start, start + size)
            bottom = slice(start + size, start + 2 * size)
            inner = dot(lower[bottom, top], inverse[top, top], HIGHEST)
            inverse[bottom, top] = -dot(inverse[bottom, bottom], inner, HIGHEST)
        size *= 2


def main_kernel(
    row_tiles, col_tiles, own_count,
    plan, own_plan, left, right, exact,
    out,
    tiles, matrix, lower0, lower1, inverse, inverse_high, inverse_low, first_high, first_low,
    panel_high, panel_low, upper_block, inverse_block,
):
    tile = matrix.shape[0]
    quadrature = right.shape[1]
    chunks = tile // ROWS
    listed = 2 + row_tiles + col_tiles
    work = plan.shape[0] // 4

    def assemble(item, chunk):
        left_index, right_index = plan[4 * item], plan[4 * item + 1]
        diagonal = plan[4 * item + 2]
        start = pl.multiple_of(chunk * ROWS, ROWS)
        wide = 2 * BLOCK
        features = left[left_index, chunk]
        offsets = lax.broadcasted_iota(jnp.int32, (ROWS, wide), 1) - lax.broadcasted_iota(
            jnp.int32, (ROWS, wide), 0
        )
        origin = jnp.where(diagonal == 1, start, 2 * tile)
        for half in range(0, tile, wide):
            here = slice(half, half + wide)
            on_diagonal = offsets == origin - half
            total = jnp.zeros((ROWS, wide), jnp.float32)
            for second in range(quadrature):
                squared = dot(features, right[right_index, second, :, here])
                for first in range(quadrature):
                    part = squared[first * ROWS : (first + 1) * ROWS]
                    if first == second:
                        same = exact[right_index, second : second + 1, here]
                        part = jnp.where(on_diagonal, same, part)
                    total = total + lax.rsqrt(part)
            shifted = exact[right_index, quadrature : quadrature + 1, here]
            tiles[item, pl.ds(start, ROWS), here] = total + jnp.where(on_diagonal, shifted, 0.0)

    def assemble_tile(item):
        def step(chunk, carry):
            assemble(item, chunk)
            return carry
        lax.fori_loop(0, chunks, step, 0)

    def side_from(first_item):
        def side(index):
            assemble(first_item + index // chunks, lax.rem(index, chunks))
        return side

    panels = tile // 8
    covered = panels // chunks
    assemble_tile(0)
    matrix[...] = tiles[0]
    factor_tile(matrix, lower0, inverse, upper_block, inverse_block, side_from(1))
    inverse_high[0], inverse_low[0] = split(inverse[...].T)

    def three(left_high, left_low, right_high, right_low, multiply):
        return (
            multiply(left_high, right_high)
            + multiply(left_high, right_low)
            + multiply(left_low, right_high)
        )

    def solve(value, step, target):
        high, low = split(value)
        half = tile // 2
        for depth, first in ((half, 0), (tile, half)):
            columns = slice(first, first + half)
            solved = three(
                high[:, :depth], low[:, :depth],
                inverse_high[step, :depth, columns], inverse_low[step, :depth, columns], dot,
            )
            into = slice(step * tile + first, step * tile + first + half)
            panel_high[target, :, into], panel_low[target, :, into] = split(solved)

    def solve_first(index, carry):
        solve(tiles[index], 0, index - 1)
        return carry

    lax.fori_loop(1, listed, solve_first, 0)
    first_high[...] = panel_high[0, :, :tile]
    first_low[...] = panel_low[0, :, :tile]

    def reduce_second(index, carry):
        update = three(
            panel_high[index - 1, :, :tile], panel_low[index - 1, :, :tile],
            first_high[...], first_low[...], dot_transposed,
        )
        item = listed - 1 + index
        tiles[item] = tiles[item] - update
        return carry

    reduce_second(1, 0)
    matrix[...] = tiles[listed]
    factor_tile(matrix, lower1, inverse, upper_block, inverse_block, side_from(1 + covered))
    inverse_high[1], inverse_low[1] = split(inverse[...].T)
    done = 1 + 2 * covered

    def solve_second(index, carry):
        reduce_second(index, carry)
        solve(tiles[listed - 1 + index], 1, index - 1)
        return carry

    lax.fori_loop(2, listed, solve_second, 0)

    def rest(item, carry):
        @pl.when(plan[4 * item + 3] == 1)
        def _():
            assemble_tile(item)
        return carry

    lax.fori_loop(done, work, rest, 0)

    lanes = tile // BLOCK
    pitch = col_tiles * lanes

    def store(i, j, value):
        for q in range(lanes):
            out[pl.ds(i * tile * pitch + j * lanes + q, tile, stride=pitch), :] = value[
                :, q * BLOCK : (q + 1) * BLOCK
            ]

    def finish(index, carry):
        i, j = index // col_tiles, lax.rem(index, col_tiles)
        kind = own_plan[2 * index]

        @pl.when(kind == 0)
        def _():
            store(i, j, jnp.zeros((tile, tile), jnp.float32))

        @pl.when(kind == 1)
        def _():
            store(i, j, lower0[...])

        @pl.when(kind == 2)
        def _():
            value = panel_high[1 + i, :, :tile].astype(jnp.float32)
            store(i, j, value + panel_low[1 + i, :, :tile].astype(jnp.float32))

        @pl.when(kind == 3)
        def _():
            store(i, j, lower1[...])

        @pl.when(kind == 4)
        def _():
            value = panel_high[1 + i, :, tile:].astype(jnp.float32)
            store(i, j, value + panel_low[1 + i, :, tile:].astype(jnp.float32))

        @pl.when(kind == 5)
        def _():
            update = three(
                panel_high[1 + i], panel_low[1 + i],
                panel_high[1 + row_tiles + j], panel_low[1 + row_tiles + j], dot_transposed,
            )
            store(i, j, tiles[own_plan[2 * index + 1]] - update)

        return carry

    lax.fori_loop(0, row_tiles * col_tiles, finish, 0)


def pieces(value):
    parts = []
    for _ in range(3):
        part = lax.reduce_precision(value, 8, 7)
        parts.append(part)
        value = value - part
    return parts


def shards(points, weights, shift, cluster_rank):
    row_count = lax.axis_size("row")
    col_count = lax.axis_size("col")
    row_index = lax.axis_index("row")
    col_index = lax.axis_index("col")
    quadrature, length = weights.shape
    clusters = cluster_rank.shape[0]
    tile = length * row_count * col_count // clusters
    row_tiles = clusters // row_count
    col_tiles = clusters // col_count

    own = jnp.concatenate([points.reshape(3 * quadrature, length), weights, shift[None]], axis=0)
    rows = own.shape[0]
    own = jnp.pad(own, ((0, -rows % 8), (0, 0)))
    everything = gather(own, row_count, col_count)

    block_rows = jnp.arange(row_tiles, dtype=jnp.int32) * row_count + row_index
    block_cols = jnp.arange(col_tiles, dtype=jnp.int32) * col_count + col_index
    places = jnp.concatenate([jnp.arange(2, dtype=jnp.int32), block_rows, block_cols])
    listed = places.shape[0]
    names = jnp.arange(clusters, dtype=jnp.int32)
    chosen = jnp.sum(
        jnp.where(cluster_rank[None, :] == places[:, None], names[None, :], 0), axis=1
    )
    everything = everything.reshape(clusters, tile // length, -1, length)
    local = jnp.take(everything, chosen, axis=0)[:, :, :rows]
    local = jnp.transpose(local, (2, 0, 1, 3)).reshape(rows, listed, tile)
    coordinates = local[: 3 * quadrature].reshape(3, quadrature, listed, tile) - 0.5
    weight = local[3 * quadrature : 4 * quadrature]
    shifted = local[4 * quadrature]
    scale = 1.0 / (weight * weight)
    norm = jnp.sum(coordinates * coordinates, axis=0)
    left_parts = pieces(
        jnp.concatenate(
            [-2.0 * coordinates * scale, ((norm + SOFTENING_SQUARED) * scale)[None], scale[None]]
        )
    )
    right_parts = pieces(
        jnp.concatenate([coordinates * scale, scale[None], (norm * scale)[None]])
    )
    pairs = [(0, 0), (0, 1), (1, 0), (1, 1), (0, 2), (2, 0)]
    left = jnp.concatenate([left_parts[i] for i, _ in pairs])
    right = jnp.concatenate([right_parts[i] for _, i in pairs])
    padding = ((0, FEATURES - left.shape[0]), (0, 0), (0, 0), (0, 0))
    left = jnp.pad(left.astype(jnp.bfloat16), padding)
    right = jnp.pad(right.astype(jnp.bfloat16), padding)
    left = left.reshape(FEATURES, quadrature, listed, tile // ROWS, ROWS)
    left = jnp.transpose(left, (2, 3, 1, 4, 0)).reshape(
        listed, tile // ROWS, quadrature * ROWS, FEATURES
    )
    right = jnp.transpose(right, (2, 1, 0, 3))
    exact = jnp.concatenate([SOFTENING_SQUARED * scale * scale, shifted[None]])
    exact = jnp.pad(jnp.transpose(exact, (1, 0, 2)), ((0, 0), (0, -exact.shape[0] % 8), (0, 0)))

    own_rows = jnp.repeat(jnp.arange(row_tiles, dtype=jnp.int32), col_tiles)
    own_cols = jnp.tile(jnp.arange(col_tiles, dtype=jnp.int32), row_tiles)
    tile_row, tile_col = block_rows[own_rows], block_cols[own_cols]
    active = (tile_row >= tile_col) & (tile_col >= 2)
    own_count = max(
        sum(
            i * row_count + r >= j * col_count + c
            for i in range(row_tiles)
            for j in range(col_tiles)
        )
        for r in range(row_count)
        for c in range(col_count)
    )
    slot = jnp.cumsum(active.astype(jnp.int32)) - 1
    takes = active[None, :] & (slot[None, :] == jnp.arange(own_count, dtype=jnp.int32)[:, None])

    def placed(values):
        return jnp.sum(jnp.where(takes, values[None, :], 0), axis=1)

    ordered = jnp.arange(1, listed, dtype=jnp.int32)
    zero = jnp.zeros((1,), jnp.int32)
    left_index = jnp.concatenate([zero, ordered, ordered, placed(own_rows + 2)])
    right_index = jnp.concatenate(
        [zero, 0 * ordered, 0 * ordered + 1, placed(own_cols + 2 + row_tiles)]
    )
    used = jnp.concatenate(
        [zero + 1, 0 * ordered + 1, 0 * ordered + 1, placed(active.astype(jnp.int32))]
    )
    diagonal = (places[left_index] == places[right_index]).astype(jnp.int32)
    plan = jnp.stack([left_index, right_index, diagonal, used], axis=1).reshape(-1)
    kind = jnp.where(
        tile_row < tile_col, 0,
        jnp.where(
            tile_col >= 2, 5,
            jnp.where(tile_col == 0, jnp.where(tile_row == 0, 1, 2), jnp.where(tile_row == 1, 3, 4)),
        ),
    ).astype(jnp.int32)
    base = 2 * listed - 1
    own_plan = jnp.stack([kind, base + jnp.where(active, slot, 0)], axis=1).reshape(-1).astype(jnp.int32)

    work = base + own_count
    whole = pl.BlockSpec(memory_space=pltpu.VMEM)
    scalars = pl.BlockSpec(memory_space=pltpu.SMEM)
    f32, bf16 = jnp.float32, jnp.bfloat16
    result = pl.pallas_call(
        functools.partial(main_kernel, row_tiles, col_tiles, own_count),
        out_shape=jax.ShapeDtypeStruct((row_tiles * tile * col_tiles * tile // BLOCK, BLOCK), f32),
        in_specs=[scalars, scalars, whole, whole, whole],
        out_specs=whole,
        scratch_shapes=[
            pltpu.VMEM((work, tile, tile), f32),
            pltpu.VMEM((tile, tile), f32),
            pltpu.VMEM((tile, tile), f32),
            pltpu.VMEM((tile, tile), f32),
            pltpu.VMEM((tile, tile), f32),
            pltpu.VMEM((2, tile, tile), bf16),
            pltpu.VMEM((2, tile, tile), bf16),
            pltpu.VMEM((tile, tile), bf16),
            pltpu.VMEM((tile, tile), bf16),
            pltpu.VMEM((listed - 1, tile, 2 * tile), bf16),
            pltpu.VMEM((listed - 1, tile, 2 * tile), bf16),
            pltpu.VMEM((BLOCK, BLOCK), f32),
            pltpu.VMEM((BLOCK, BLOCK), f32),
        ],
        compiler_params=pltpu.CompilerParams(vmem_limit_bytes=63 * 1024 * 1024),
        name="assemble_and_factor",
    )(plan, own_plan, left, right, exact)
    return result.reshape(row_tiles, 1, tile, col_tiles, 1, tile)


def solution(mesh):
    return jax.shard_map(
        shards,
        mesh=mesh,
        in_specs=(P(None, None, ("row", "col")), P(None, ("row", "col")), P(("row", "col")), P()),
        out_specs=P(None, "row", None, None, "col", None),
        check_vma=False,
    )
```
